32 devices in a mesh: fsdp: 4 (over y, core), replica: 8 (over z, x).
Axes of the slice: x: 2, y: 2, z: 4, core: 2. Of those that a mesh axis runs over, the one named last changes fastest.
Arguments:
- acts: bfloat16 [8, 1024, 4096], P('replica', 'fsdp'), may hold values from -6 to 6
- cotangent: bfloat16 [8, 1024, 512], P('replica', 'fsdp'), may hold values from -0.5 to 0.5
- weight: float32 [8, 4096, 512], P('replica', 'fsdp'), may hold values from -0.09375 to 0.09375
- first_moment: bfloat16 [8, 4096, 512], P('replica', 'fsdp'), may hold values from -6 to 6
- second_moment: bfloat16 [8, 4096, 512], P('replica', 'fsdp'), may hold values from 0.25 to 4
- outer_weight: float32 [4096, 128], P('fsdp'), may hold values from -0.09375 to 0.09375
- outer_momentum: float32 [4096, 128], P('fsdp'), may hold values from -4 to 4
- mantissas: int32 [8, 4096, 128], P('replica', 'fsdp'), may hold values from -127 to 127
- exponents: int32 [8, 4096], P('replica', 'fsdp'), may hold values from -10 to -3, as said below
Outputs:
- weight_out: float32 [8, 4096, 512], P('replica', 'fsdp')
- first_out: bfloat16 [8, 4096, 512], P('replica', 'fsdp')
- second_out: bfloat16 [8, 4096, 512], P('replica', 'fsdp')
- outer_out: float32 [4096, 128], P('fsdp')
- momentum_out: float32 [4096, 128], P('fsdp')
The draws below stay inside these ranges and needn't reach their ends.
Inputs may be any that keep to these rules, and one draw needn't show every extreme that they name: `exponents`: in every row d exactly one island holds the largest exponent.
All inputs are finite; a program needn't handle non-finite values.
Results may differ from the reference program's by a relative error of at most 0.0055.
Values may be sent and summed in bfloat16 or wider, within the bound.
No kernel may reach another device: no remote copies, remote signals or barrier semaphores. Data moves between devices by JAX's collectives and lax.ppermute only.
A program may use at most 64 MiB of HBM per device.

```python
import math
import jax
import jax.numpy as jnp
from jax import lax

D = 4096
HD = 128
KVW = 512
TOK_ISL = 1024
N_REPLICA = 8


def draw_exponents(key, part):
    base_level = jax.random.randint(jax.random.fold_in(key, 11), (D,), -6, -2)
    owner_ids = jax.random.randint(jax.random.fold_in(key, 12), (D,), 0, N_REPLICA)
    drop_size = jax.random.randint(jax.random.fold_in(key, 13), (N_REPLICA, D), 1, 5)
    replica_ids = lax.broadcasted_iota(jnp.int32, (N_REPLICA, D), 0)
    return jnp.where(replica_ids == owner_ids[None, :], base_level[None, :], base_level[None, :] - drop_size).astype(jnp.int32)


def plant(result, key, least, high):
    index_at = [jax.random.randint(jax.random.fold_in(key, axis), (), 0, length) for axis, length in enumerate(result.shape)]
    main_axis = result.shape.index(max(result.shape))
    neighbour = index_at[:main_axis] + [(index_at[main_axis] + 1) % result.shape[main_axis]] + index_at[main_axis + 1:]
    return result.at[tuple(index_at)].set(least).at[tuple(neighbour)].set(high)


def shard_levels(rng, shape, shards, low, largest):
    level = 1.0
    for axis_at, shards_of in shards:
        steps = jax.random.uniform(jax.random.fold_in(jax.random.fold_in(rng, 6), axis_at), (shards_of,), jnp.float32, low / len(shards), largest / len(shards))
        level = level * jnp.repeat(jnp.exp(steps), shape[axis_at] // shards_of).reshape((-1,) + (1,) * (len(shape) - 1 - axis_at))
    return level


def scatter_about(key, shape, deviation, bound, pieces=(), held_as=jnp.bfloat16):
    loudness = shard_levels(key, shape, pieces, -0.22, 0.18) if pieces else 1.0
    result = jax.random.normal(key, shape, jnp.float32) * deviation * loudness
    return jnp.minimum(jnp.maximum(result, -bound), bound).astype(held_as)


def setup_inputs(seed: int = 0) -> dict:
    key_of = jax.random.split(jax.random.key(seed), 10)
    return {
        "acts": scatter_about(key_of[0], (N_REPLICA, TOK_ISL, D), 1.0, 6.0, ((0, 8), (1, 4))),
        "cotangent": scatter_about(key_of[1], (N_REPLICA, TOK_ISL, KVW), 0.03125, 0.5, ((0, 8), (1, 4))),
        "weight": scatter_about(key_of[2], (N_REPLICA, D, KVW), D ** -0.5, 0.09375, ((0, 8), (1, 4)), jnp.float32),
        "first_moment": scatter_about(key_of[3], (N_REPLICA, D, KVW), 1.0, 6.0, ((0, 8), (1, 4))),
        "second_moment": jnp.clip(jnp.exp(math.log(4.0) - 2.7725887 * jax.random.uniform(key_of[4], (N_REPLICA, D, KVW), jnp.float32) ** shard_levels(key_of[4], (N_REPLICA, D, KVW), ((0, 8), (1, 4)), -0.2, 0.2)), 0.25, 4.0).astype(jnp.bfloat16),
        "outer_weight": scatter_about(key_of[5], (D, HD), D ** -0.5, 0.09375, ((0, 4),), jnp.float32),
        "outer_momentum": scatter_about(key_of[6], (D, HD), 0.5, 4.0, ((0, 4),), jnp.float32),
        "mantissas": plant(jax.random.randint(key_of[7], (N_REPLICA, D, HD), -127, 128), jax.random.fold_in(key_of[7], 1), -127, 127).astype(jnp.int32),
        "exponents": draw_exponents(jax.random.fold_in(key_of[9], 71), 0),
    }


BETA_ONE = 0.9
BETA_TWO = 0.95
LEARN_RATE = 0.001
DECAY_RATE = 0.1
ADAM_EPSILON = 1e-08
OUTER_RATE = 0.7
OUTER_MOMENTUM = 0.9
MIX_SHARE = 0.5

def reference(acts, cotangent, weight, first_moment, second_moment, outer_weight, outer_momentum, mantissas, exponents):
    shared = lax.optimization_barrier(jnp.max(exponents, axis=0))
    aligned = jnp.right_shift(mantissas, (shared[None, :] - exponents)[:, :, None])
    summed = lax.optimization_barrier(jnp.sum(aligned, axis=0, dtype=jnp.int32))
    pseudo = summed.astype(jnp.float32) * jnp.exp2(shared.astype(jnp.float32))[:, None] / N_REPLICA
    momentum_new = OUTER_MOMENTUM * outer_momentum + pseudo
    outer_new = outer_weight - OUTER_RATE * (pseudo + OUTER_MOMENTUM * momentum_new)

    def island(island_args):
        tokens, cot_rows, weight_rows, first_rows, second_rows = island_args
        gradient = jnp.dot(tokens.T, cot_rows, preferred_element_type=jnp.float32)
        moment_one = BETA_ONE * first_rows.astype(jnp.float32) + (1.0 - BETA_ONE) * gradient
        moment_two = BETA_TWO * second_rows.astype(jnp.float32) + (1.0 - BETA_TWO) * gradient * gradient
        updated = weight_rows - LEARN_RATE * (moment_one / (jnp.sqrt(moment_two) + ADAM_EPSILON) + DECAY_RATE * weight_rows)
        head_part = MIX_SHARE * updated[:, :HD] + (1.0 - MIX_SHARE) * outer_new
        mixed = jnp.concatenate([head_part, updated[:, HD:]], axis=1)
        return (mixed, moment_one.astype(jnp.bfloat16), moment_two.astype(jnp.bfloat16))
    weight_out, first_out, second_out = lax.map(island, (acts, cotangent, weight, first_moment, second_moment))
    return (weight_out, first_out, second_out, outer_new, momentum_new)
```

```python
import functools

import jax
import jax.numpy as jnp
from jax import lax
from jax.experimental import pallas as pl
from jax.experimental.pallas import tpu as pltpu
from jax.sharding import PartitionSpec as P

BETA_ONE = 0.9
BETA_TWO = 0.95
LEARN_RATE = 0.001
DECAY_RATE = 0.1
ADAM_EPSILON = 1e-08
OUTER_RATE = 0.7
OUTER_MOMENTUM = 0.9
MIX_SHARE = 0.5
LEAST_EXPONENT = -10

ANY = pl.BlockSpec(memory_space=pl.ANY)
VMEM = pl.BlockSpec(memory_space=pltpu.VMEM)
LIMIT = 32 * 1024 * 1024
PIECE = 256


def params():
    return pltpu.CompilerParams(vmem_limit_bytes=LIMIT)


def token_product(tokens, cot):
    return lax.dot_general(tokens, cot, (((0,), (0,)), ((), ())), preferred_element_type=jnp.float32)


def load_columns(acts_ref, buf, sems, first):
    copies = []
    for i in range(buf.shape[0]):
        width = buf.shape[2]
        cols = pl.ds(pl.multiple_of(first + i * width, 128), width)
        copies.append(pltpu.make_async_copy(acts_ref.at[:, cols], buf.at[i], sems.at[i]))
        copies[-1].start()
    return copies


def partial_kernel(flip, row, rows, acts_ref, cot_ref, out_ref, buf, sems):
    owner = lax.axis_index("fsdp") ^ flip
    copies = load_columns(acts_ref, buf, sems, owner * rows + row)
    for i, copy in enumerate(copies):
        copy.wait()
        out_ref[i * PIECE:(i + 1) * PIECE, :] = token_product(buf[i], cot_ref[...]).astype(out_ref.dtype)


def partial_sum_kernel(flip, row, rows, acts_ref, cot_ref, other_ref, out_ref, buf, sems):
    owner = lax.axis_index("fsdp") ^ flip
    copies = load_columns(acts_ref, buf, sems, owner * rows + row)
    for i, copy in enumerate(copies):
        copy.wait()
        at = slice(i * PIECE, (i + 1) * PIECE)
        total = token_product(buf[i], cot_ref[...]) + other_ref[at, :].astype(jnp.float32)
        out_ref[at, :] = total.astype(out_ref.dtype)


def partial(acts, cot, flip, row, count, rows, dtype, other=None):
    tokens, width = cot.shape
    kernel = partial_kernel if other is None else partial_sum_kernel
    operands = (acts, cot) + (() if other is None else (other,))
    return pl.pallas_call(
        functools.partial(kernel, flip, row, rows),
        out_shape=jax.ShapeDtypeStruct((count, width), dtype),
        in_specs=[ANY] + [VMEM] * (len(operands) - 1),
        out_specs=VMEM,
        scratch_shapes=[
            pltpu.VMEM((count // PIECE, tokens, PIECE), acts.dtype),
            pltpu.SemaphoreType.DMA((count // PIECE,)),
        ],
        compiler_params=params(),
        cost_estimate=pl.CostEstimate(
            flops=2 * count * tokens * width, bytes_accessed=2 * count * (tokens + width), transcendentals=0
        ),
    )(*operands)


def adam_kernel(own_ref, core_ref, chip_ref, weight_ref, first_ref, second_ref, *rest):
    weight_out, first_out, second_out = rest[-3:]
    gradient = own_ref[...] + core_ref[...].astype(jnp.float32) + chip_ref[...].astype(jnp.float32)
    moment_one = BETA_ONE * first_ref[...].astype(jnp.float32) + (1.0 - BETA_ONE) * gradient
    moment_two = BETA_TWO * second_ref[...].astype(jnp.float32) + (1.0 - BETA_TWO) * gradient * gradient
    weight = weight_ref[...]
    weight_out[...] = weight - LEARN_RATE * (
        moment_one / (jnp.sqrt(moment_two) + ADAM_EPSILON) + DECAY_RATE * weight
    )
    first_out[...] = moment_one.astype(first_out.dtype)
    second_out[...] = moment_two.astype(second_out.dtype)


def adam(own, core, chip, weight, first, second, row, outs):
    block = 128
    rows, width = weight.shape
    count = chip.shape[0]
    here = pl.BlockSpec((block, width), lambda i: (row // block + i, 0))
    operands = [own, core, chip, weight, first, second]
    specs = [here, here, pl.BlockSpec((block, width), lambda i: (i, 0)), here, here, here]
    aliases = {}
    if outs is not None:
        aliases = {len(operands) + i: i for i in range(3)}
        operands += list(outs)
        specs += [ANY] * 3
    return pl.pallas_call(
        adam_kernel,
        out_shape=[jax.ShapeDtypeStruct(a.shape, a.dtype) for a in (weight, first, second)],
        grid=(count // block,),
        in_specs=specs,
        out_specs=[here] * 3,
        input_output_aliases=aliases,
        compiler_params=params(),
        cost_estimate=pl.CostEstimate(
            flops=20 * count * width, bytes_accessed=24 * count * width, transcendentals=2 * count * width
        ),
    )(*operands)


def by_row(exps_ref, at):
    line = exps_ref[pl.ds(at, 1), :]
    return jnp.broadcast_to(line, (128, 128)).T


def code_kernel(parts, group, mant_ref, *refs):
    exps, outs = refs[: len(refs) - parts], refs[len(refs) - parts:]
    where = lax.axis_index("replica") // group
    length = outs[0].shape[0]
    for k in range(parts):
        row = (where ^ k) * length
        for i in range(length // 128):
            line = row // 128 + i
            own = by_row(exps[0], line)
            top = own
            for other in exps[1:]:
                top = jnp.maximum(top, by_row(other, line))
            mant = mant_ref[pl.ds(pl.multiple_of(row + i * 128, 128), 128), :]
            code = mant * 64 + (own - LEAST_EXPONENT) * 8 + (top - LEAST_EXPONENT)
            outs[k][i * 128:(i + 1) * 128, :] = code.astype(outs[k].dtype)


def align_kernel(*refs):
    codes = [r[...].astype(jnp.int32) for r in refs[:-1]]
    top = functools.reduce(jnp.maximum, [c & 7 for c in codes])
    total = sum(jnp.right_shift(c >> 6, top - ((c >> 3) & 7)) for c in codes)
    refs[-1][...] = (total * 8 + top).astype(refs[-1].dtype)


def outer_kernel(group, islands, weight_in, ow_ref, om_ref, *refs):
    parts = len(refs) - 6
    codes = refs[:parts]
    weight_out, outer_out, momentum_out, head, load_sem, store_sems = refs[parts:]
    where = lax.axis_index("replica") // group
    length = codes[0].shape[0]
    width = head.shape[1]
    load = pltpu.make_async_copy(weight_out.at[:, pl.ds(0, width)], head, load_sem)
    load.start()
    load.wait()
    for k in range(parts):
        at = pl.ds(pl.multiple_of((where ^ k) * length, length), length)
        code = codes[k][...].astype(jnp.int32)
        scale = jnp.left_shift(1, code & 7).astype(jnp.float32) * (2.0 ** LEAST_EXPONENT / islands)
        pseudo = (code >> 3).astype(jnp.float32) * scale
        momentum = OUTER_MOMENTUM * om_ref[at, :] + pseudo
        outer = ow_ref[at, :] - OUTER_RATE * (pseudo + OUTER_MOMENTUM * momentum)
        momentum_out[at, :] = momentum
        outer_out[at, :] = outer
        head[at, :] = MIX_SHARE * head[at, :] + (1.0 - MIX_SHARE) * outer
    store = pltpu.make_async_copy(head, weight_out.at[:, pl.ds(0, width)], store_sems)
    store.start()
    store.wait()


def outer_step(weight, outer_weight, outer_momentum, codes, group, islands):
    return pl.pallas_call(
        functools.partial(outer_kernel, group, islands),
        out_shape=[jax.ShapeDtypeStruct(a.shape, a.dtype) for a in (weight, outer_weight, outer_momentum)],
        in_specs=[ANY] + [VMEM] * (2 + len(codes)),
        out_specs=[ANY, VMEM, VMEM],
        input_output_aliases={0: 0},
        scratch_shapes=[
            pltpu.VMEM(outer_weight.shape, jnp.float32),
            pltpu.SemaphoreType.DMA,
            pltpu.SemaphoreType.DMA,
        ],
        compiler_params=params(),
    )(weight, outer_weight, outer_momentum, *codes)


def swap(x, axis, flip):
    size = lax.axis_size(axis)
    return lax.ppermute(x, axis, [(i, i ^ flip) for i in range(size)])


def island_groups(islands):
    inner = 2
    while inner * inner * 4 <= islands:
        inner *= 2
    return islands // inner, inner


def fragment_codes(mant, exps):
    islands = lax.axis_size("replica")
    parts, group = island_groups(islands)
    rows, head = mant.shape
    length = rows // parts
    lines = exps.reshape(rows // 128, 128)
    all_lines = [lines] + [swap(lines, "replica", k) for k in range(1, group)]
    codes = pl.pallas_call(
        functools.partial(code_kernel, parts, group),
        out_shape=[jax.ShapeDtypeStruct((length, head), jnp.int16)] * parts,
        in_specs=[VMEM] * (1 + group),
        out_specs=[VMEM] * parts,
        compiler_params=params(),
    )(mant, *all_lines)
    codes = [codes[0]] + [swap(codes[k], "replica", k * group) for k in range(1, parts)]
    wide = jnp.int16 if islands * 128 * 8 <= 2 ** 15 else jnp.int32
    code = pl.pallas_call(
        align_kernel,
        out_shape=jax.ShapeDtypeStruct((length, head), wide),
        in_specs=[VMEM] * parts,
        out_specs=VMEM,
        compiler_params=params(),
    )(*codes)
    total = code
    for k in range(1, group):
        total = total + (swap(code, "replica", k) & -8)
    return [total] + [swap(total, "replica", k * group) for k in range(1, parts)], group, islands


def local(acts, cotangent, weight, first, second, outer_weight, outer_momentum, mantissas, exponents):
    acts, cot, weight, first, second = acts[0], cotangent[0], weight[0], first[0], second[0]
    rows, width = weight.shape
    bf16 = jnp.bfloat16
    chunks = ((0, rows // 4), (rows // 4, rows // 2), (3 * rows // 4, rows // 4))

    codes, group, islands = fragment_codes(mantissas[0], exponents[0])

    theirs = [partial(acts, cot, 3, row, count, rows, bf16) for row, count in chunks]
    theirs = [swap(part, "fsdp", 1) for part in theirs]
    sends = [
        partial(acts, cot, 2, row, count, rows, bf16, other)
        for (row, count), other in zip(chunks, theirs)
    ]
    arrived = [swap(part, "fsdp", 2) for part in sends]
    core = swap(partial(acts, cot, 1, 0, rows, rows, bf16), "fsdp", 1)
    own = partial(acts, cot, 0, 0, rows, rows, jnp.float32)
    outs = None
    for (row, _), part in zip(chunks, arrived):
        outs = adam(own, core, part, weight, first, second, row, outs)
    weight_new, first_new, second_new = outs
    weight_new, outer_new, momentum_new = outer_step(
        weight_new, outer_weight, outer_momentum, codes, group, islands
    )
    return (weight_new[None], first_new[None], second_new[None], outer_new, momentum_new)


def solution(mesh):
    tall = P("replica", "fsdp", None)
    fragment = P("fsdp", None)
    in_specs = (tall, tall, tall, tall, tall, fragment, fragment, tall, P("replica", "fsdp"))
    out_specs = (tall, tall, tall, fragment, fragment)
    return jax.shard_map(local, mesh=mesh, in_specs=in_specs, out_specs=out_specs, check_vma=False)
```

```python
import functools

import jax
import jax.numpy as jnp
from jax import lax
from jax.experimental import pallas as pl
from jax.experimental.pallas import tpu as pltpu
from jax.sharding import PartitionSpec as P

BETA_ONE = 0.9
BETA_TWO = 0.95
LEARN_RATE = 0.001
DECAY_RATE = 0.1
ADAM_EPSILON = 1e-08
OUTER_RATE = 0.7
OUTER_MOMENTUM = 0.9
MIX_SHARE = 0.5
LEAST_EXPONENT = -10

ANY = pl.BlockSpec(memory_space=pl.ANY)
VMEM = pl.BlockSpec(memory_space=pltpu.VMEM)
COST = (0, 0, 0, 5)
OPT = (1, 0)
UNITS = (2, 3, 3)
FILL = (0, 20, 20, 20, 20, 20)
LIMIT = 32 * 1024 * 1024


def params():
    return pltpu.CompilerParams(vmem_limit_bytes=LIMIT)


def cost(us):
    return pl.CostEstimate(flops=int(us * 1.15e9), bytes_accessed=0, transcendentals=0)


def token_product(tokens, cot):
    return lax.dot_general(tokens, cot, (((0,), (0,)), ((), ())), preferred_element_type=jnp.float32)


def product_kernel(flip, row, rows, summed, acts_ref, cot_ref, *refs):
    out_ref, buf, cot, sems, cot_sem = refs[-5:]
    owner = lax.axis_index("fsdp") ^ flip
    cot_copy = pltpu.make_async_copy(cot_ref, cot, cot_sem)
    cot_copy.start()
    pieces, _, width = buf.shape
    copies = []
    for i in range(pieces):
        cols = pl.ds(pl.multiple_of(owner * rows + row + i * width, 128), width)
        copies.append(pltpu.make_async_copy(acts_ref.at[:, cols], buf.at[i], sems.at[i]))
        copies[-1].start()
    cot_copy.wait()
    for i, copy in enumerate(copies):
        copy.wait()
        at = slice(i * width, (i + 1) * width)
        total = token_product(buf[i], cot[...])
        if summed:
            total = total + refs[0][at, :].astype(jnp.float32)
        out_ref[at, :] = total.astype(out_ref.dtype)


def product(acts, cot, flip, row, count, rows, dtype, other=None, after=(), us=0):
    tokens, width = cot.shape
    piece = next(p for p in (256, 384, 128, count) if count % p == 0)
    shares = () if other is None else (other,)
    return pl.pallas_call(
        functools.partial(product_kernel, flip, row, rows, len(shares)),
        out_shape=jax.ShapeDtypeStruct((count, width), dtype),
        in_specs=[ANY, ANY] + [VMEM] * len(shares) + [ANY] * len(after),
        out_specs=VMEM,
        scratch_shapes=[
            pltpu.VMEM((count // piece, tokens, piece), acts.dtype),
            pltpu.VMEM(cot.shape, cot.dtype),
            pltpu.SemaphoreType.DMA((count // piece,)),
            pltpu.SemaphoreType.DMA,
        ],
        compiler_params=params(),
        cost_estimate=cost(us),
    )(acts, cot, *shares, *after)


def adam_step(gradient, weight, first, second):
    moment_one = BETA_ONE * first.astype(jnp.float32) + (1.0 - BETA_ONE) * gradient
    moment_two = BETA_TWO * second.astype(jnp.float32) + (1.0 - BETA_TWO) * gradient * gradient
    updated = weight - LEARN_RATE * (
        moment_one / (jnp.sqrt(moment_two) + ADAM_EPSILON) + DECAY_RATE * weight
    )
    return updated, moment_one.astype(first.dtype), moment_two.astype(second.dtype)


def adam_kernel(own_ref, core_ref, chip_ref, weight_ref, first_ref, second_ref, *rest):
    weight_out, first_out, second_out, head_out = rest[-4:]
    gradient = own_ref[...] + core_ref[...].astype(jnp.float32) + chip_ref[...].astype(jnp.float32)
    weight_out[...], first_out[...], second_out[...] = adam_step(
        gradient, weight_ref[...], first_ref[...], second_ref[...]
    )
    head_out[...] = weight_out[:, : head_out.shape[1]]


def adam(own, core, chip, weight, first, second, row, head, outs=(), us=0, after=()):
    block = 128
    rows, width = weight.shape
    count = chip.shape[0]
    here = pl.BlockSpec((block, width), lambda i: (row // block + i, 0))
    operands = [own, core, chip, weight, first, second]
    specs = [here, here, pl.BlockSpec((block, width), lambda i: (i, 0)), here, here, here]
    aliases = {len(operands) + i: i for i in range(len(outs))}
    operands += list(outs)
    operands += list(after)
    specs += [ANY] * (len(outs) + len(after))
    return pl.pallas_call(
        adam_kernel,
        out_shape=[jax.ShapeDtypeStruct(a.shape, a.dtype) for a in (weight, first, second)]
        + [jax.ShapeDtypeStruct((count, head), weight.dtype)],
        grid=(count // block,),
        in_specs=specs,
        out_specs=[here] * 3 + [pl.BlockSpec((block, head), lambda i: (i, 0))],
        input_output_aliases=aliases,
        compiler_params=params(),
        cost_estimate=cost(us),
    )(*operands)


def by_row(exps_ref, at):
    line = exps_ref[pl.ds(at, 1), :]
    return jnp.broadcast_to(line, (128, 128)).T


def code_kernel(parts, group, mant_ref, *refs):
    exps, outs = refs[:group], refs[len(refs) - parts:]
    where = lax.axis_index("replica") // group
    length = outs[0].shape[0]
    for k in range(parts):
        row = (where ^ k) * length
        for i in range(length // 128):
            line = row // 128 + i
            own = by_row(exps[0], line)
            top = own
            for other in exps[1:]:
                top = jnp.maximum(top, by_row(other, line))
            mant = mant_ref[pl.ds(pl.multiple_of(row + i * 128, 128), 128), :]
            code = mant * 64 + (own - LEAST_EXPONENT) * 8 + (top - LEAST_EXPONENT)
            outs[k][i * 128:(i + 1) * 128, :] = code.astype(outs[k].dtype)


def align_kernel(parts, *refs):
    codes = [r[...].astype(jnp.int32) for r in refs[:parts]]
    top = functools.reduce(jnp.maximum, [c & 7 for c in codes])
    total = sum(jnp.right_shift(c >> 6, top - ((c >> 3) & 7)) for c in codes)
    refs[-1][...] = (total * 8 + top).astype(refs[-1].dtype)


def finish_kernel(group, islands, parts, early, *refs):
    weight_ref, first_ref, second_ref, own_ref, core_ref, chip_ref, ow_ref, om_ref = refs[:8]
    codes, heads = refs[8:8 + parts], refs[8 + parts:8 + parts + early]
    weight_out, first_out, second_out, outer_out, momentum_out = refs[8 + parts + early + 3:-7]
    weight_new, first_new, second_new, outer, momentum, mixed, sems = refs[-7:]
    where = lax.axis_index("replica") // group
    length = codes[0].shape[0]
    count = chip_ref.shape[0]
    last = weight_ref.shape[0] - count
    width = mixed.shape[1]
    stores = []

    def store(source, target):
        stores.append(pltpu.make_async_copy(source, target, sems.at[len(stores)]))
        stores[-1].start()

    for k in range(parts):
        at = pl.ds(pl.multiple_of((where ^ k) * length, length), length)
        code = codes[k][...].astype(jnp.int32)
        scale = jnp.left_shift(1, code & 7).astype(jnp.float32) * (2.0 ** LEAST_EXPONENT / islands)
        pseudo = (code >> 3).astype(jnp.float32) * scale
        moved = OUTER_MOMENTUM * om_ref[at, :] + pseudo
        momentum[at, :] = moved
        outer[at, :] = ow_ref[at, :] - OUTER_RATE * (pseudo + OUTER_MOMENTUM * moved)
    store(momentum, momentum_out)
    store(outer, outer_out)
    row = 0
    for head in heads:
        at = slice(row, row + head.shape[0])
        mixed[at, :] = MIX_SHARE * head[...] + (1.0 - MIX_SHARE) * outer[at, :]
        row += head.shape[0]
    store(mixed, weight_out.at[pl.ds(0, last), pl.ds(0, width)])
    block = 128
    for i in range(count // block):
        here, there = slice(i * block, (i + 1) * block), slice(last + i * block, last + (i + 1) * block)
        gradient = own_ref[there, :] + core_ref[there, :].astype(jnp.float32) + chip_ref[here, :].astype(jnp.float32)
        updated, first_new[here, :], second_new[here, :] = adam_step(
            gradient, weight_ref[there, :], first_ref[there, :], second_ref[there, :]
        )
        weight_new[here, width:] = updated[:, width:]
        weight_new[here, :width] = MIX_SHARE * updated[:, :width] + (1.0 - MIX_SHARE) * outer[there, :]
        for new, out in ((weight_new, weight_out), (first_new, first_out), (second_new, second_out)):
            store(new.at[pl.ds(i * block, block)], out.at[pl.ds(last + i * block, block)])
    for copy in stores:
        copy.wait()


def finish(weight, first, second, own, core, chip, outer_weight, outer_momentum, codes, heads, outs, group, islands):
    parts, early = len(codes), len(heads)
    count, width = chip.shape
    fragment = outer_weight.shape
    operands = [weight, first, second, own, core, chip, outer_weight, outer_momentum, *codes, *heads]
    return pl.pallas_call(
        functools.partial(finish_kernel, group, islands, parts, early),
        out_shape=[
            jax.ShapeDtypeStruct(a.shape, a.dtype) for a in (weight, first, second, outer_weight, outer_momentum)
        ],
        in_specs=[VMEM] * len(operands) + [ANY] * 3,
        out_specs=[ANY] * 5,
        input_output_aliases={len(operands) + i: i for i in range(3)},
        scratch_shapes=[
            pltpu.VMEM((count, width), weight.dtype),
            pltpu.VMEM((count, width), first.dtype),
            pltpu.VMEM((count, width), second.dtype),
            pltpu.VMEM(fragment, jnp.float32),
            pltpu.VMEM(fragment, jnp.float32),
            pltpu.VMEM((weight.shape[0] - count, fragment[1]), jnp.float32),
            pltpu.SemaphoreType.DMA((3 + 3 * (count // 128),)),
        ],
        compiler_params=params(),
        cost_estimate=cost(0),
    )(*operands, *outs)


def swap(x, axis, flip):
    size = lax.axis_size(axis)
    return lax.ppermute(x, axis, [(i, i ^ flip) for i in range(size)])


def island_groups(islands):
    inner = 2
    while inner * inner * 4 <= islands:
        inner *= 2
    return islands // inner, inner


def copy_kernel(x_ref, out_ref):
    out_ref[...] = x_ref[...]


def held(x, us):
    return pl.pallas_call(
        copy_kernel,
        out_shape=jax.ShapeDtypeStruct(x.shape, x.dtype),
        in_specs=[VMEM],
        out_specs=VMEM,
        compiler_params=params(),
        cost_estimate=cost(us),
    )(x)


def join_kernel(others, code_ref, *refs):
    total = code_ref[...]
    for other in refs[:others]:
        total += other[...] & -8
    refs[-1][...] = total


def local(acts, cotangent, weight, first, second, outer_weight, outer_momentum, mantissas, exponents):
    acts, cot, weight, first, second = acts[0], cotangent[0], weight[0], first[0], second[0]
    mant, lines = mantissas[0], exponents[0].reshape(-1, 128)
    rows, width = weight.shape
    bf16 = jnp.bfloat16
    islands = lax.axis_size("replica")
    parts, group = island_groups(islands)
    length, head = rows // parts, mant.shape[1]
    unit = rows // 8
    chunks, row = [], 0
    for units in UNITS:
        chunks.append((row * unit, units * unit))
        row += units

    lines = held(lines, COST[3])
    all_lines = [lines] + [swap(lines, "replica", k) for k in range(1, group)]
    first_part = all_lines[1:] if OPT[1] else all_lines[:1]
    theirs = []
    for row, count in chunks:
        theirs.append(
            product(acts, cot, 3, row, count, rows, bf16, after=theirs[-1:] or first_part, us=FILL[3] if theirs else 0)
        )
    shares = [swap(part, "fsdp", 1) for part in theirs]
    sends = []
    for n, ((row, count), other) in enumerate(zip(chunks, shares)):
        sends.append(
            product(acts, cot, 2, row, count, rows, bf16, other, after=sends[-1:] or theirs[-1:], us=FILL[5 if n > 1 else 4])
        )
    arrived = [swap(part, "fsdp", 2) for part in sends]

    codes = pl.pallas_call(
        functools.partial(code_kernel, parts, group),
        out_shape=[jax.ShapeDtypeStruct((length, head), jnp.int16)] * parts,
        in_specs=[VMEM] * (1 + group) + [ANY],
        out_specs=[VMEM] * parts,
        compiler_params=params(),
        cost_estimate=cost(COST[0]),
    )(mant, *all_lines, sends[OPT[0]])
    core = product(acts, cot, 1, 0, rows, rows, bf16, after=codes[:1], us=FILL[0])
    codes = [codes[0]] + [swap(codes[k], "replica", k * group) for k in range(1, parts)]
    wide = jnp.int16 if islands * 128 * 8 <= 2 ** 15 else jnp.int32
    code = pl.pallas_call(
        functools.partial(align_kernel, parts),
        out_shape=jax.ShapeDtypeStruct((length, head), wide),
        in_specs=[VMEM] * parts + [ANY] * 2,
        out_specs=VMEM,
        compiler_params=params(),
        cost_estimate=cost(0),
    )(*codes, core, sends[-1])
    core = swap(core, "fsdp", 1)
    others = [swap(code, "replica", k) for k in range(1, group)]
    own = product(acts, cot, 0, 0, rows, rows, jnp.float32, after=(code,), us=FILL[1])
    *outs, part_head = adam(own, core, arrived[0], weight, first, second, 0, head, us=FILL[1], after=(code,))
    heads = [part_head]
    total = pl.pallas_call(
        functools.partial(join_kernel, group - 1),
        out_shape=jax.ShapeDtypeStruct((length, head), wide),
        in_specs=[VMEM] * group + [ANY],
        out_specs=VMEM,
        compiler_params=params(),
        cost_estimate=cost(0),
    )(code, *others, part_head)
    codes = [total] + [swap(total, "replica", k * group) for k in range(1, parts)]
    for (row, _), part in zip(chunks[1:-1], arrived[1:]):
        *outs, part_head = adam(own, core, part, weight, first, second, row, head, outs, us=FILL[2])
        heads.append(part_head)
    weight_new, first_new, second_new, outer_new, momentum_new = finish(
        weight, first, second, own, core, arrived[-1], outer_weight, outer_momentum, codes, heads, outs, group, islands
    )
    return (weight_new[None], first_new[None], second_new[None], outer_new, momentum_new)


def solution(mesh):
    tall = P("replica", "fsdp", None)
    fragment = P("fsdp", None)
    in_specs = (tall, tall, tall, tall, tall, fragment, fragment, tall, P("replica", "fsdp"))
    out_specs = (tall, tall, tall, fragment, fragment)
    return jax.shard_map(local, mesh=mesh, in_specs=in_specs, out_specs=out_specs, check_vma=False)
```

```python
import functools

import jax
import jax.numpy as jnp
from jax import lax
from jax.experimental import pallas as pl
from jax.experimental.pallas import tpu as pltpu
from jax.sharding import PartitionSpec as P

BETA_ONE = 0.9
BETA_TWO = 0.95
LEARN_RATE = 0.001
DECAY_RATE = 0.1
ADAM_EPSILON = 1e-08
OUTER_RATE = 0.7
OUTER_MOMENTUM = 0.9
MIX_SHARE = 0.5
LEAST_EXPONENT = -10

ANY = pl.BlockSpec(memory_space=pl.ANY)
VMEM = pl.BlockSpec(memory_space=pltpu.VMEM)
COST = (0, 0, 0, 1)
OPT = (1, 0, 0)
UNITS = (2, 4, 2)
FILL = (0, 20, 20, 20, 20, 20)
LIMIT = 32 * 1024 * 1024


def params():
    return pltpu.CompilerParams(vmem_limit_bytes=LIMIT)


def cost(us):
    return pl.CostEstimate(flops=int(us * 1.15e9), bytes_accessed=0, transcendentals=0)


def token_product(tokens, cot):
    return lax.dot_general(tokens, cot, (((0,), (0,)), ((), ())), preferred_element_type=jnp.float32)


def pieces(count):
    size = next(s for s in (256, 384, 128) if count % s == 0)
    return [(at, size) for at in range(0, count, size)]


def product_kernel(flip, row, rows, summed, skip, acts_ref, cot_ref, *refs):
    out_ref, buf, cot, sems, cot_sem = refs[-5:]
    owner = lax.axis_index("fsdp") ^ flip
    cot_copy = pltpu.make_async_copy(cot_ref, cot, cot_sem)
    cot_copy.start()
    copies = []
    for n, (at, size) in enumerate(pieces(out_ref.shape[0])):
        cols = pl.ds(pl.multiple_of(owner * rows + row + at, 128), size)
        copies.append(pltpu.make_async_copy(acts_ref.at[:, cols], buf.at[:, pl.ds(at, size)], sems.at[n]))
        copies[-1].start()
    cot_copy.wait()
    for copy, (at, size) in zip(copies, pieces(out_ref.shape[0])):
        copy.wait()
        total = token_product(buf[:, at:at + size], cot[...])
        if summed:
            total = total + refs[0][skip + at:skip + at + size, :].astype(jnp.float32)
        out_ref[at:at + size, :] = total.astype(out_ref.dtype)


def product(acts, cot, flip, row, count, rows, dtype, other=None, skip=0, after=(), us=0):
    tokens, width = cot.shape
    shares = () if other is None else (other,)
    return pl.pallas_call(
        functools.partial(product_kernel, flip, row, rows, len(shares), skip),
        out_shape=jax.ShapeDtypeStruct((count, width), dtype),
        in_specs=[ANY, ANY] + [VMEM] * len(shares) + [ANY] * len(after),
        out_specs=VMEM,
        scratch_shapes=[
            pltpu.VMEM((tokens, count), acts.dtype),
            pltpu.VMEM(cot.shape, cot.dtype),
            pltpu.SemaphoreType.DMA((len(pieces(count)),)),
            pltpu.SemaphoreType.DMA,
        ],
        compiler_params=params(),
        cost_estimate=cost(us),
    )(acts, cot, *shares, *after)


def adam_step(gradient, weight, first, second):
    moment_one = BETA_ONE * first.astype(jnp.float32) + (1.0 - BETA_ONE) * gradient
    moment_two = BETA_TWO * second.astype(jnp.float32) + (1.0 - BETA_TWO) * gradient * gradient
    updated = weight - LEARN_RATE * (
        moment_one / (jnp.sqrt(moment_two) + ADAM_EPSILON) + DECAY_RATE * weight
    )
    return updated, moment_one.astype(first.dtype), moment_two.astype(second.dtype)


def adam_kernel(own_ref, core_ref, chip_ref, weight_ref, first_ref, second_ref, *rest):
    weight_out, first_out, second_out, head_out = rest[-4:]
    gradient = own_ref[...] + core_ref[...].astype(jnp.float32) + chip_ref[...].astype(jnp.float32)
    weight_out[...], first_out[...], second_out[...] = adam_step(
        gradient, weight_ref[...], first_ref[...], second_ref[...]
    )
    head_out[...] = weight_out[:, : head_out.shape[1]]


def adam(own, core, chip, weight, first, second, row, head, outs=(), us=0, after=()):
    block = 128
    rows, width = weight.shape
    count = chip.shape[0]
    here = pl.BlockSpec((block, width), lambda i: (row // block + i, 0))
    operands = [own, core, chip, weight, first, second]
    specs = [here, here, pl.BlockSpec((block, width), lambda i: (i, 0)), here, here, here]
    aliases = {len(operands) + i: i for i in range(len(outs))}
    operands += list(outs)
    operands += list(after)
    specs += [ANY] * (len(outs) + len(after))
    return pl.pallas_call(
        adam_kernel,
        out_shape=[jax.ShapeDtypeStruct(a.shape, a.dtype) for a in (weight, first, second)]
        + [jax.ShapeDtypeStruct((count, head), weight.dtype)],
        grid=(count // block,),
        in_specs=specs,
        out_specs=[here] * 3 + [pl.BlockSpec((block, head), lambda i: (i, 0))],
        input_output_aliases=aliases,
        compiler_params=params(),
        cost_estimate=cost(us),
    )(*operands)


def by_row(exps_ref, at):
    line = exps_ref[pl.ds(at, 1), :]
    return jnp.broadcast_to(line, (128, 128)).T


def code_kernel(parts, group, mant_ref, *refs):
    exps, outs = refs[:group], refs[len(refs) - parts:]
    where = lax.axis_index("replica") // group
    length = outs[0].shape[0]
    for k in range(parts):
        row = (where ^ k) * length
        for i in range(length // 128):
            line = row // 128 + i
            own = by_row(exps[0], line)
            top = own
            for other in exps[1:]:
                top = jnp.maximum(top, by_row(other, line))
            mant = mant_ref[pl.ds(pl.multiple_of(row + i * 128, 128), 128), :]
            code = mant * 64 + (own - LEAST_EXPONENT) * 8 + (top - LEAST_EXPONENT)
            outs[k][i * 128:(i + 1) * 128, :] = code.astype(outs[k].dtype)


def align_kernel(parts, *refs):
    codes = [r[...].astype(jnp.int32) for r in refs[:parts]]
    top = functools.reduce(jnp.maximum, [c & 7 for c in codes])
    total = sum(jnp.right_shift(c >> 6, top - ((c >> 3) & 7)) for c in codes)
    refs[-1][...] = (total * 8 + top).astype(refs[-1].dtype)


def finish_kernel(group, islands, parts, early, *refs):
    weight_ref, first_ref, second_ref, own_ref, core_ref, chip_ref, ow_ref, om_ref = refs[:8]
    codes, heads = refs[8:8 + parts], refs[8 + parts:8 + parts + early]
    weight_out, first_out, second_out, outer_out, momentum_out = refs[8 + parts + early + 3:-7]
    weight_new, first_new, second_new, outer, momentum, mixed, sems = refs[-7:]
    where = lax.axis_index("replica") // group
    length = codes[0].shape[0]
    count = chip_ref.shape[0]
    last = weight_ref.shape[0] - count
    width = mixed.shape[1]
    stores = []

    def store(source, target):
        stores.append(pltpu.make_async_copy(source, target, sems.at[len(stores)]))
        stores[-1].start()

    for k in range(parts):
        at = pl.ds(pl.multiple_of((where ^ k) * length, length), length)
        code = codes[k][...].astype(jnp.int32)
        scale = jnp.left_shift(1, code & 7).astype(jnp.float32) * (2.0 ** LEAST_EXPONENT / islands)
        pseudo = (code >> 3).astype(jnp.float32) * scale
        moved = OUTER_MOMENTUM * om_ref[at, :] + pseudo
        momentum[at, :] = moved
        outer[at, :] = ow_ref[at, :] - OUTER_RATE * (pseudo + OUTER_MOMENTUM * moved)
        store(momentum.at[at], momentum_out.at[at])
        store(outer.at[at], outer_out.at[at])
    row = 0
    for head in heads:
        at = slice(row, row + head.shape[0])
        mixed[at, :] = MIX_SHARE * head[...] + (1.0 - MIX_SHARE) * outer[at, :]
        row += head.shape[0]
    store(mixed, weight_out.at[pl.ds(0, last), pl.ds(0, width)])
    block = 128
    for i in range(count // block):
        here, there = slice(i * block, (i + 1) * block), slice(last + i * block, last + (i + 1) * block)
        gradient = own_ref[there, :] + core_ref[there, :].astype(jnp.float32) + chip_ref[here, :].astype(jnp.float32)
        updated, first_new[here, :], second_new[here, :] = adam_step(
            gradient, weight_ref[there, :], first_ref[there, :], second_ref[there, :]
        )
        weight_new[here, width:] = updated[:, width:]
        weight_new[here, :width] = MIX_SHARE * updated[:, :width] + (1.0 - MIX_SHARE) * outer[there, :]
        for new, out in ((weight_new, weight_out), (first_new, first_out), (second_new, second_out)):
            store(new.at[pl.ds(i * block, block)], out.at[pl.ds(last + i * block, block)])
    for copy in stores:
        copy.wait()


def finish(weight, first, second, own, core, chip, outer_weight, outer_momentum, codes, heads, outs, group, islands):
    parts, early = len(codes), len(heads)
    count, width = chip.shape
    fragment = outer_weight.shape
    operands = [weight, first, second, own, core, chip, outer_weight, outer_momentum, *codes, *heads]
    return pl.pallas_call(
        functools.partial(finish_kernel, group, islands, parts, early),
        out_shape=[
            jax.ShapeDtypeStruct(a.shape, a.dtype) for a in (weight, first, second, outer_weight, outer_momentum)
        ],
        in_specs=[VMEM] * len(operands) + [ANY] * 3,
        out_specs=[ANY] * 5,
        input_output_aliases={len(operands) + i: i for i in range(3)},
        scratch_shapes=[
            pltpu.VMEM((count, width), weight.dtype),
            pltpu.VMEM((count, width), first.dtype),
            pltpu.VMEM((count, width), second.dtype),
            pltpu.VMEM(fragment, jnp.float32),
            pltpu.VMEM(fragment, jnp.float32),
            pltpu.VMEM((weight.shape[0] - count, fragment[1]), jnp.float32),
            pltpu.SemaphoreType.DMA((2 * parts + 1 + 3 * (count // 128),)),
        ],
        compiler_params=params(),
        cost_estimate=cost(0),
    )(*operands, *outs)


def swap(x, axis, flip):
    size = lax.axis_size(axis)
    return lax.ppermute(x, axis, [(i, i ^ flip) for i in range(size)])


def island_groups(islands):
    inner = 2
    while inner * inner * 4 <= islands:
        inner *= 2
    return islands // inner, inner


def add_kernel(mine_ref, other_ref, out_ref):
    out_ref[...] = (mine_ref[...] + other_ref[...].astype(jnp.float32)).astype(out_ref.dtype)


def start_kernel(out_ref):
    out_ref[...] = jnp.zeros_like(out_ref)


def join_kernel(others, code_ref, *refs):
    total = code_ref[...]
    for other in refs[:others]:
        total += other[...] & -8
    refs[-1][...] = total


def local(acts, cotangent, weight, first, second, outer_weight, outer_momentum, mantissas, exponents):
    acts, cot, weight, first, second = acts[0], cotangent[0], weight[0], first[0], second[0]
    mant, lines = mantissas[0], exponents[0].reshape(-1, 128)
    rows, width = weight.shape
    bf16 = jnp.bfloat16
    islands = lax.axis_size("replica")
    parts, group = island_groups(islands)
    length, head = rows // parts, mant.shape[1]
    unit = rows // 8
    chunks, row = [], 0
    for units in UNITS:
        chunks.append((row * unit, units * unit))
        row += units

    ready = pl.pallas_call(
        start_kernel,
        out_shape=jax.ShapeDtypeStruct((8, 128), jnp.int32),
        out_specs=VMEM,
        compiler_params=params(),
        cost_estimate=cost(COST[3]),
    )()
    all_lines = [lines] + [swap(lines, "replica", k) for k in range(1, group)]

    first_count, rest = chunks[0][1], rows - chunks[0][1]
    theirs = [product(acts, cot, 3, 0, first_count, rows, bf16, after=(ready,))]
    shares = [swap(theirs[0], "fsdp", 1)]
    if OPT[0]:
        theirs.append(product(acts, cot, 3, first_count, rest, rows, bf16, after=theirs, us=FILL[3]))

    mine = product(acts, cot, 2, 0, first_count, rows, jnp.float32, after=theirs[-1:], us=FILL[4])
    sends = [
        pl.pallas_call(
            add_kernel,
            out_shape=jax.ShapeDtypeStruct(mine.shape, bf16),
            in_specs=[VMEM, VMEM],
            out_specs=VMEM,
            compiler_params=params(),
            cost_estimate=cost(0),
        )(mine, shares[0])
    ]
    codes = pl.pallas_call(
        functools.partial(code_kernel, parts, group),
        out_shape=[jax.ShapeDtypeStruct((length, head), jnp.int16)] * parts,
        in_specs=[VMEM] * (1 + group) + [ANY],
        out_specs=[VMEM] * parts,
        compiler_params=params(),
        cost_estimate=cost(COST[0]),
    )(mant, *all_lines, sends[0])
    if not OPT[0]:
        theirs.append(product(acts, cot, 3, first_count, rest, rows, bf16, after=sends[:1], us=FILL[3]))
    shares.append(swap(theirs[1], "fsdp", 1))
    for n, (row, count) in enumerate(chunks[1:]):
        sends.append(
            product(acts, cot, 2, row, count, rows, bf16, shares[1], row - first_count, after=sends[-1:], us=FILL[5])
        )
    arrived = [swap(part, "fsdp", 2) for part in sends]
    core = product(acts, cot, 1, 0, rows, rows, bf16, after=sends[1:2], us=FILL[0])
    if OPT[1]:
        own = product(acts, cot, 0, 0, rows, rows, jnp.float32, after=(core,))
    codes = list(codes)
    for k in (1,):
        codes[k], _ = lax.optimization_barrier((codes[k], sends[1]))
    codes = [codes[0]] + [swap(codes[k], "replica", k * group) for k in range(parts - 1, 0, -1)]
    wide = jnp.int16 if islands * 128 * 8 <= 2 ** 15 else jnp.int32
    code = pl.pallas_call(
        functools.partial(align_kernel, parts),
        out_shape=jax.ShapeDtypeStruct((length, head), wide),
        in_specs=[VMEM] * parts + [ANY] * 2,
        out_specs=VMEM,
        compiler_params=params(),
        cost_estimate=cost(0),
    )(*codes, own if OPT[1] else core, sends[-1])
    core = swap(core, "fsdp", 1)
    others = [swap(code, "replica", k) for k in range(1, group)]
    if not OPT[1]:
        own = product(acts, cot, 0, 0, rows, rows, jnp.float32, after=(code,), us=FILL[1])
    *outs, part_head = adam(own, core, arrived[0], weight, first, second, 0, head, us=FILL[1], after=(code,))
    heads = [part_head]
    total = pl.pallas_call(
        functools.partial(join_kernel, group - 1),
        out_shape=jax.ShapeDtypeStruct((length, head), wide),
        in_specs=[VMEM] * group + [ANY],
        out_specs=VMEM,
        compiler_params=params(),
        cost_estimate=cost(0),
    )(code, *others, own if OPT[2] else part_head)
    codes = [total] + [swap(total, "replica", k * group) for k in range(1, parts)]
    for (row, _), part in zip(chunks[1:-1], arrived[1:]):
        *outs, part_head = adam(own, core, part, weight, first, second, row, head, outs, us=FILL[2])
        heads.append(part_head)
    weight_new, first_new, second_new, outer_new, momentum_new = finish(
        weight, first, second, own, core, arrived[-1], outer_weight, outer_momentum, codes, heads, outs, group, islands
    )
    return (weight_new[None], first_new[None], second_new[None], outer_new, momentum_new)


def solution(mesh):
    tall = P("replica", "fsdp", None)
    fragment = P("fsdp", None)
    in_specs = (tall, tall, tall, tall, tall, fragment, fragment, tall, P("replica", "fsdp"))
    out_specs = (tall, tall, tall, fragment, fragment)
    return jax.shard_map(local, mesh=mesh, in_specs=in_specs, out_specs=out_specs, check_vma=False)
```

```python
import functools

import jax
import jax.numpy as jnp
from jax import lax
from jax.experimental import pallas as pl
from jax.experimental.pallas import tpu as pltpu
from jax.sharding import PartitionSpec as P

BETA_ONE = 0.9
BETA_TWO = 0.95
LEARN_RATE = 0.001
DECAY_RATE = 0.1
ADAM_EPSILON = 1e-08
OUTER_RATE = 0.7
OUTER_MOMENTUM = 0.9
MIX_SHARE = 0.5
LEAST_EXPONENT = -10

ANY = pl.BlockSpec(memory_space=pl.ANY)
VMEM = pl.BlockSpec(memory_space=pltpu.VMEM)
BLOCK = 128
FILL = 20
LIMIT = 32 * 1024 * 1024


def params():
    return pltpu.CompilerParams(vmem_limit_bytes=LIMIT)


def cost(us):
    return pl.CostEstimate(flops=int(us * 1.15e9), bytes_accessed=0, transcendentals=0)


def token_product(tokens, cot):
    return lax.dot_general(tokens, cot, (((0,), (0,)), ((), ())), preferred_element_type=jnp.float32)


def product_kernel(flip, row, rows, summed, skip, acts_ref, cot_ref, *refs):
    out_ref = refs[-1]
    owner = lax.axis_index("fsdp") ^ flip
    for at in range(0, out_ref.shape[0], 128):
        size = min(128, out_ref.shape[0] - at)
        cols = pl.ds(pl.multiple_of(owner * rows + row + at, 128), size)
        total = token_product(acts_ref[:, cols], cot_ref[...])
        if summed:
            total = total + refs[0][skip + at:skip + at + size, :].astype(jnp.float32)
        out_ref[at:at + size, :] = total.astype(out_ref.dtype)


def product(acts, cot, flip, row, count, rows, dtype, other=None, skip=0, after=(), us=0):
    width = cot.shape[1]
    shares = () if other is None else (other,)
    return pl.pallas_call(
        functools.partial(product_kernel, flip, row, rows, len(shares), skip),
        out_shape=jax.ShapeDtypeStruct((count, width), dtype),
        in_specs=[VMEM] * (2 + len(shares)) + [ANY] * len(after),
        out_specs=VMEM,
        compiler_params=params(),
        cost_estimate=cost(us),
    )(acts, cot, *shares, *after)


def adam_step(gradient, weight, first, second):
    moment_one = BETA_ONE * first.astype(jnp.float32) + (1.0 - BETA_ONE) * gradient
    moment_two = BETA_TWO * second.astype(jnp.float32) + (1.0 - BETA_TWO) * gradient * gradient
    updated = weight - LEARN_RATE * (
        moment_one / (jnp.sqrt(moment_two) + ADAM_EPSILON) + DECAY_RATE * weight
    )
    return updated, moment_one.astype(first.dtype), moment_two.astype(second.dtype)


def adam_kernel(own_ref, core_ref, chip_ref, weight_ref, first_ref, second_ref, *rest):
    weight_out, first_out, second_out, head_out = rest[-4:]
    gradient = own_ref[...] + core_ref[...].astype(jnp.float32) + chip_ref[...].astype(jnp.float32)
    weight_out[...], first_out[...], second_out[...] = adam_step(
        gradient, weight_ref[...], first_ref[...], second_ref[...]
    )
    head_out[...] = weight_out[:, : head_out.shape[1]]


def adam(own, core, chip, weight, first, second, row, head, outs=(), us=0, after=()):
    block = 128
    rows, width = weight.shape
    count = chip.shape[0]
    here = pl.BlockSpec((block, width), lambda i: (row // block + i, 0))
    operands = [own, core, chip, weight, first, second]
    specs = [here, here, pl.BlockSpec((block, width), lambda i: (i, 0)), here, here, here]
    aliases = {len(operands) + i: i for i in range(len(outs))}
    operands += list(outs)
    operands += list(after)
    specs += [ANY] * (len(outs) + len(after))
    return pl.pallas_call(
        adam_kernel,
        out_shape=[jax.ShapeDtypeStruct(a.shape, a.dtype) for a in (weight, first, second)]
        + [jax.ShapeDtypeStruct((count, head), weight.dtype)],
        grid=(count // BLOCK,),
        in_specs=specs,
        out_specs=[here] * 3 + [pl.BlockSpec((block, head), lambda i: (i, 0))],
        input_output_aliases=aliases,
        compiler_params=params(),
        cost_estimate=cost(us),
    )(*operands)


def by_row(exps_ref, at):
    line = exps_ref[pl.ds(at, 1), :]
    return jnp.broadcast_to(line, (128, 128)).T


def code_kernel(parts, group, mant_ref, *refs):
    exps, outs = refs[:group], refs[len(refs) - parts:]
    where = lax.axis_index("replica") // group
    length = outs[0].shape[0]
    for k in range(parts):
        row = (where ^ k) * length
        for i in range(length // 128):
            line = row // 128 + i
            own = by_row(exps[0], line)
            top = own
            for other in exps[1:]:
                top = jnp.maximum(top, by_row(other, line))
            mant = mant_ref[pl.ds(pl.multiple_of(row + i * 128, 128), 128), :]
            code = mant * 64 + (own - LEAST_EXPONENT) * 8 + (top - LEAST_EXPONENT)
            outs[k][i * 128:(i + 1) * 128, :] = code.astype(outs[k].dtype)


def align_kernel(parts, *refs):
    codes = [r[...].astype(jnp.int32) for r in refs[:parts]]
    top = functools.reduce(jnp.maximum, [c & 7 for c in codes])
    total = sum(jnp.right_shift(c >> 6, top - ((c >> 3) & 7)) for c in codes)
    refs[-1][...] = (total * 8 + top).astype(refs[-1].dtype)


def finish_kernel(group, islands, parts, early, *refs):
    weight_ref, first_ref, second_ref, own_ref, core_ref, chip_ref, ow_ref, om_ref = refs[:8]
    codes, heads = refs[8:8 + parts], refs[8 + parts:8 + parts + early]
    weight_out, first_out, second_out, outer_out, momentum_out = refs[8 + parts + early + 3:-7]
    weight_new, first_new, second_new, outer, momentum, mixed, sems = refs[-7:]
    where = lax.axis_index("replica") // group
    length = codes[0].shape[0]
    count = chip_ref.shape[0]
    last = weight_ref.shape[0] - count
    width = mixed.shape[1]
    stores = []

    def store(source, target):
        stores.append(pltpu.make_async_copy(source, target, sems.at[len(stores)]))
        stores[-1].start()

    for k in range(parts):
        at = pl.ds(pl.multiple_of((where ^ k) * length, length), length)
        code = codes[k][...].astype(jnp.int32)
        scale = jnp.left_shift(1, code & 7).astype(jnp.float32) * (2.0 ** LEAST_EXPONENT / islands)
        pseudo = (code >> 3).astype(jnp.float32) * scale
        moved = OUTER_MOMENTUM * om_ref[at, :] + pseudo
        momentum[at, :] = moved
        outer[at, :] = ow_ref[at, :] - OUTER_RATE * (pseudo + OUTER_MOMENTUM * moved)
        store(momentum.at[at], momentum_out.at[at])
        store(outer.at[at], outer_out.at[at])
    row = 0
    for head in heads:
        at = slice(row, row + head.shape[0])
        mixed[at, :] = MIX_SHARE * head[...] + (1.0 - MIX_SHARE) * outer[at, :]
        row += head.shape[0]
    store(mixed, weight_out.at[pl.ds(0, last), pl.ds(0, width)])
    for i in range(count // BLOCK):
        here, there = slice(i * BLOCK, (i + 1) * BLOCK), slice(last + i * BLOCK, last + (i + 1) * BLOCK)
        gradient = own_ref[there, :] + core_ref[there, :].astype(jnp.float32) + chip_ref[here, :].astype(jnp.float32)
        updated, first_new[here, :], second_new[here, :] = adam_step(
            gradient, weight_ref[there, :], first_ref[there, :], second_ref[there, :]
        )
        weight_new[here, width:] = updated[:, width:]
        weight_new[here, :width] = MIX_SHARE * updated[:, :width] + (1.0 - MIX_SHARE) * outer[there, :]
        for new, out in ((weight_new, weight_out), (first_new, first_out), (second_new, second_out)):
            store(new.at[pl.ds(i * BLOCK, BLOCK)], out.at[pl.ds(last + i * BLOCK, BLOCK)])
    for copy in stores:
        copy.wait()


def finish(weight, first, second, own, core, chip, outer_weight, outer_momentum, codes, heads, outs, group, islands):
    parts, early = len(codes), len(heads)
    count, width = chip.shape
    fragment = outer_weight.shape
    operands = [weight, first, second, own, core, chip, outer_weight, outer_momentum, *codes, *heads]
    return pl.pallas_call(
        functools.partial(finish_kernel, group, islands, parts, early),
        out_shape=[
            jax.ShapeDtypeStruct(a.shape, a.dtype) for a in (weight, first, second, outer_weight, outer_momentum)
        ],
        in_specs=[VMEM] * len(operands) + [ANY] * 3,
        out_specs=[ANY] * 5,
        input_output_aliases={len(operands) + i: i for i in range(3)},
        scratch_shapes=[
            pltpu.VMEM((count, width), weight.dtype),
            pltpu.VMEM((count, width), first.dtype),
            pltpu.VMEM((count, width), second.dtype),
            pltpu.VMEM(fragment, jnp.float32),
            pltpu.VMEM(fragment, jnp.float32),
            pltpu.VMEM((weight.shape[0] - count, fragment[1]), jnp.float32),
            pltpu.SemaphoreType.DMA((2 * parts + 1 + 3 * (count // BLOCK),)),
        ],
        compiler_params=params(),
        cost_estimate=cost(0),
    )(*operands, *outs)


def swap(x, axis, flip):
    size = lax.axis_size(axis)
    return lax.ppermute(x, axis, [(i, i ^ flip) for i in range(size)])


def island_groups(islands):
    inner = 2
    while inner * inner * 4 <= islands:
        inner *= 2
    return islands // inner, inner


def add_kernel(mine_ref, other_ref, out_ref):
    out_ref[...] = (mine_ref[...] + other_ref[...].astype(jnp.float32)).astype(out_ref.dtype)


def start_kernel(out_ref):
    out_ref[...] = jnp.zeros_like(out_ref)


def join_kernel(others, code_ref, *refs):
    total = code_ref[...]
    for other in refs[:others]:
        total += other[...] & -8
    refs[-1][...] = total


def local(acts, cotangent, weight, first, second, outer_weight, outer_momentum, mantissas, exponents):
    acts, cot, weight, first, second = acts[0], cotangent[0], weight[0], first[0], second[0]
    mant, lines = mantissas[0], exponents[0].reshape(-1, 128)
    rows, width = weight.shape
    bf16 = jnp.bfloat16
    islands = lax.axis_size("replica")
    parts, group = island_groups(islands)
    length, head = rows // parts, mant.shape[1]
    unit = rows // 8
    chunks = ((0, 2 * unit), (2 * unit, 4 * unit), (6 * unit, 2 * unit))
    late = rows - chunks[0][1]

    ready = pl.pallas_call(
        start_kernel,
        out_shape=jax.ShapeDtypeStruct((8, 128), jnp.int32),
        out_specs=VMEM,
        compiler_params=params(),
        cost_estimate=cost(1),
    )()
    all_lines = [lines] + [swap(lines, "replica", k) for k in range(1, group)]

    theirs = [product(acts, cot, 3, *chunks[0], rows, bf16, after=(ready,))]
    theirs.append(product(acts, cot, 3, chunks[1][0], late, rows, bf16, after=theirs, us=FILL))
    shares = [swap(part, "fsdp", 1) for part in theirs]
    mine = product(acts, cot, 2, *chunks[0], rows, jnp.float32, after=theirs[1:], us=FILL)
    sends = [
        pl.pallas_call(
            add_kernel,
            out_shape=jax.ShapeDtypeStruct(mine.shape, bf16),
            in_specs=[VMEM, VMEM],
            out_specs=VMEM,
            compiler_params=params(),
            cost_estimate=cost(0),
        )(mine, shares[0])
    ]
    codes = pl.pallas_call(
        functools.partial(code_kernel, parts, group),
        out_shape=[jax.ShapeDtypeStruct((length, head), jnp.int16)] * parts,
        in_specs=[VMEM] * (1 + group) + [ANY],
        out_specs=[VMEM] * parts,
        compiler_params=params(),
        cost_estimate=cost(0),
    )(mant, *all_lines, sends[0])
    for row, count in chunks[1:]:
        sends.append(
            product(acts, cot, 2, row, count, rows, bf16, shares[1], row - chunks[1][0], after=sends[-1:], us=FILL)
        )
    arrived = [swap(part, "fsdp", 2) for part in sends]

    core = product(acts, cot, 1, 0, rows, rows, bf16, after=sends[1:2])
    codes = list(codes)
    codes[1], _ = lax.optimization_barrier((codes[1], sends[1]))
    codes = codes[:1] + [swap(codes[k], "replica", k * group) for k in range(parts - 1, 0, -1)]
    wide = jnp.int16 if islands * 128 * 8 <= 2 ** 15 else jnp.int32
    code = pl.pallas_call(
        functools.partial(align_kernel, parts),
        out_shape=jax.ShapeDtypeStruct((length, head), wide),
        in_specs=[VMEM] * parts + [ANY] * 2,
        out_specs=VMEM,
        compiler_params=params(),
        cost_estimate=cost(0),
    )(*codes, core, sends[2])
    core = swap(core, "fsdp", 1)
    others = [swap(code, "replica", k) for k in range(1, group)]
    own = product(acts, cot, 0, 0, rows, rows, jnp.float32, after=(code,), us=FILL)
    total = pl.pallas_call(
        functools.partial(join_kernel, group - 1),
        out_shape=jax.ShapeDtypeStruct((length, head), wide),
        in_specs=[VMEM] * group + [ANY],
        out_specs=VMEM,
        compiler_params=params(),
        cost_estimate=cost(0),
    )(code, *others, own)
    received = {k: swap(total, "replica", k * group) for k in range(parts - 1, 0, -1)}
    codes = [total] + [received[k] for k in range(1, parts)]

    outs, heads = (), []
    for (row, _), part in zip(chunks[:-1], arrived):
        *outs, part_head = adam(
            own, core, part, weight, first, second, row, head, outs, us=FILL, after=() if outs else (total,)
        )
        heads.append(part_head)
    weight_new, first_new, second_new, outer_new, momentum_new = finish(
        weight, first, second, own, core, arrived[-1], outer_weight, outer_momentum, codes, heads, outs, group, islands
    )
    return (weight_new[None], first_new[None], second_new[None], outer_new, momentum_new)


def solution(mesh):
    tall = P("replica", "fsdp", None)
    fragment = P("fsdp", None)
    in_specs = (tall, tall, tall, tall, tall, fragment, fragment, tall, P("replica", "fsdp"))
    out_specs = (tall, tall, tall, fragment, fragment)
    return jax.shard_map(local, mesh=mesh, in_specs=in_specs, out_specs=out_specs, check_vma=False)
```

```python
import functools

import jax
import jax.numpy as jnp
from jax import lax
from jax.experimental import pallas as pl
from jax.experimental.pallas import tpu as pltpu
from jax.sharding import PartitionSpec as P

BETA_ONE = 0.9
BETA_TWO = 0.95
LEARN_RATE = 0.001
DECAY_RATE = 0.1
ADAM_EPSILON = 1e-08
OUTER_RATE = 0.7
OUTER_MOMENTUM = 0.9
MIX_SHARE = 0.5
LEAST_EXPONENT = -10

ANY = pl.BlockSpec(memory_space=pl.ANY)
VMEM = pl.BlockSpec(memory_space=pltpu.VMEM)
BLOCK = 128
FILL = 20
LIMIT = 32 * 1024 * 1024


def params():
    return pltpu.CompilerParams(vmem_limit_bytes=LIMIT)


def cost(us):
    return pl.CostEstimate(flops=int(us * 1.15e9), bytes_accessed=0, transcendentals=0)


def token_product(tokens, cot):
    return lax.dot_general(tokens, cot, (((0,), (0,)), ((), ())), preferred_element_type=jnp.float32)


def product_kernel(flip, row, rows, summed, skip, acts_ref, cot_ref, *refs):
    out_ref = refs[-1]
    owner = lax.axis_index("fsdp") ^ flip
    for at in range(0, out_ref.shape[0], 128):
        size = min(128, out_ref.shape[0] - at)
        cols = pl.ds(pl.multiple_of(owner * rows + row + at, 128), size)
        total = token_product(acts_ref[:, cols], cot_ref[...])
        if summed:
            total = total + refs[0][skip + at:skip + at + size, :].astype(jnp.float32)
        out_ref[at:at + size, :] = total.astype(out_ref.dtype)


def product(acts, cot, flip, row, count, rows, dtype, other=None, skip=0, after=(), us=0):
    width = cot.shape[1]
    shares = () if other is None else (other,)
    return pl.pallas_call(
        functools.partial(product_kernel, flip, row, rows, len(shares), skip),
        out_shape=jax.ShapeDtypeStruct((count, width), dtype),
        in_specs=[VMEM] * (2 + len(shares)) + [ANY] * len(after),
        out_specs=VMEM,
        compiler_params=params(),
        cost_estimate=cost(us),
    )(acts, cot, *shares, *after)


def adam_step(gradient, weight, first, second):
    moment_one = BETA_ONE * first.astype(jnp.float32) + (1.0 - BETA_ONE) * gradient
    moment_two = BETA_TWO * second.astype(jnp.float32) + (1.0 - BETA_TWO) * gradient * gradient
    root = moment_two * lax.rsqrt(moment_two)
    step = moment_one / (root + ADAM_EPSILON)
    updated = weight - LEARN_RATE * (step + DECAY_RATE * weight)
    return updated, moment_one.astype(first.dtype), moment_two.astype(second.dtype)


def adam_kernel(row, own_ref, core_ref, chip_ref, weight_ref, first_ref, second_ref, *refs):
    weight_out, first_out, second_out, head_out, weight_new, first_new, second_new, sems = refs[-8:]
    count = chip_ref.shape[0]
    stores = []
    for i in range(count // BLOCK):
        here, there = slice(i * BLOCK, (i + 1) * BLOCK), slice(row + i * BLOCK, row + (i + 1) * BLOCK)
        gradient = own_ref[there, :] + core_ref[there, :].astype(jnp.float32) + chip_ref[here, :].astype(jnp.float32)
        updated, first_new[here, :], second_new[here, :] = adam_step(
            gradient, weight_ref[there, :], first_ref[there, :], second_ref[there, :]
        )
        weight_new[here, :] = updated
        head_out[here, :] = updated[:, : head_out.shape[1]]
        for new, out in ((weight_new, weight_out), (first_new, first_out), (second_new, second_out)):
            stores.append(
                pltpu.make_async_copy(
                    new.at[pl.ds(i * BLOCK, BLOCK)], out.at[pl.ds(row + i * BLOCK, BLOCK)], sems.at[len(stores)]
                )
            )
            stores[-1].start()
    for copy in stores:
        copy.wait()


def adam(own, core, chip, weight, first, second, row, head, outs=(), us=0, after=()):
    count, width = chip.shape
    operands = [own, core, chip, weight, first, second]
    return pl.pallas_call(
        functools.partial(adam_kernel, row),
        out_shape=[jax.ShapeDtypeStruct(a.shape, a.dtype) for a in (weight, first, second)]
        + [jax.ShapeDtypeStruct((count, head), weight.dtype)],
        in_specs=[VMEM] * len(operands) + [ANY] * (len(outs) + len(after)),
        out_specs=[ANY] * 3 + [VMEM],
        input_output_aliases={len(operands) + i: i for i in range(len(outs))},
        scratch_shapes=[
            pltpu.VMEM((count, width), weight.dtype),
            pltpu.VMEM((count, width), first.dtype),
            pltpu.VMEM((count, width), second.dtype),
            pltpu.SemaphoreType.DMA((3 * (count // BLOCK),)),
        ],
        compiler_params=params(),
        cost_estimate=cost(us),
    )(*operands, *outs, *after)


def by_row(exps_ref, at):
    line = exps_ref[pl.ds(at, 1), :]
    return jnp.broadcast_to(line, (128, 128)).T


def code_kernel(parts, group, mant_ref, *refs):
    exps, outs = refs[:group], refs[len(refs) - parts:]
    where = lax.axis_index("replica") // group
    length = outs[0].shape[0]
    for k in range(parts):
        row = (where ^ k) * length
        for i in range(length // 128):
            line = row // 128 + i
            own = by_row(exps[0], line)
            top = own
            for other in exps[1:]:
                top = jnp.maximum(top, by_row(other, line))
            mant = mant_ref[pl.ds(pl.multiple_of(row + i * 128, 128), 128), :]
            code = mant * 64 + (own - LEAST_EXPONENT) * 8 + (top - LEAST_EXPONENT)
            outs[k][i * 128:(i + 1) * 128, :] = code.astype(outs[k].dtype)


def align_kernel(parts, *refs):
    codes = [r[...].astype(jnp.int32) for r in refs[:parts]]
    top = functools.reduce(jnp.maximum, [c & 7 for c in codes])
    total = sum(jnp.right_shift(c >> 6, top - ((c >> 3) & 7)) for c in codes)
    refs[-1][...] = (total * 8 + top).astype(refs[-1].dtype)


def outer_kernel(group, islands, parts, early, ow_ref, om_ref, *refs):
    codes, heads = refs[:parts], refs[parts:parts + early]
    weight_out, outer_out, momentum_out, tail_out, outer, momentum, mixed, sems = refs[parts + early + 1:]
    where = lax.axis_index("replica") // group
    length = codes[0].shape[0]
    last, width = mixed.shape
    stores = []

    def store(source, target):
        stores.append(pltpu.make_async_copy(source, target, sems.at[len(stores)]))
        stores[-1].start()

    for k in range(parts):
        at = pl.ds(pl.multiple_of((where ^ k) * length, length), length)
        code = codes[k][...].astype(jnp.int32)
        scale = jnp.left_shift(1, code & 7).astype(jnp.float32) * (2.0 ** LEAST_EXPONENT / islands)
        pseudo = (code >> 3).astype(jnp.float32) * scale
        moved = OUTER_MOMENTUM * om_ref[at, :] + pseudo
        momentum[at, :] = moved
        outer[at, :] = ow_ref[at, :] - OUTER_RATE * (pseudo + OUTER_MOMENTUM * moved)
        store(momentum.at[at], momentum_out.at[at])
        store(outer.at[at], outer_out.at[at])
    row = 0
    for head in heads:
        at = slice(row, row + head.shape[0])
        mixed[at, :] = MIX_SHARE * head[...] + (1.0 - MIX_SHARE) * outer[at, :]
        row += head.shape[0]
    store(mixed, weight_out.at[pl.ds(0, last), pl.ds(0, width)])
    tail_out[...] = outer[last:, :]
    for copy in stores:
        copy.wait()


def outer_step(weight, outer_weight, outer_momentum, codes, heads, group, islands):
    parts, early = len(codes), len(heads)
    rows, width = outer_weight.shape
    last = sum(h.shape[0] for h in heads)
    operands = [outer_weight, outer_momentum, *codes, *heads]
    return pl.pallas_call(
        functools.partial(outer_kernel, group, islands, parts, early),
        out_shape=[jax.ShapeDtypeStruct(a.shape, a.dtype) for a in (weight, outer_weight, outer_momentum)]
        + [jax.ShapeDtypeStruct((rows - last, width), jnp.float32)],
        in_specs=[VMEM] * len(operands) + [ANY],
        out_specs=[ANY] * 3 + [VMEM],
        input_output_aliases={len(operands): 0},
        scratch_shapes=[
            pltpu.VMEM((rows, width), jnp.float32),
            pltpu.VMEM((rows, width), jnp.float32),
            pltpu.VMEM((last, width), jnp.float32),
            pltpu.SemaphoreType.DMA((2 * parts + 1,)),
        ],
        compiler_params=params(),
        cost_estimate=cost(0),
    )(*operands, weight)


def last_kernel(weight_ref, first_ref, second_ref, own_ref, core_ref, chip_ref, outer_ref, *refs):
    weight_out, first_out, second_out, weight_new, first_new, second_new, sems = refs[3:]
    count = chip_ref.shape[0]
    last = weight_ref.shape[0] - count
    width = outer_ref.shape[1]
    stores = []
    for i in range(count // BLOCK):
        here, there = slice(i * BLOCK, (i + 1) * BLOCK), slice(last + i * BLOCK, last + (i + 1) * BLOCK)
        gradient = own_ref[there, :] + core_ref[there, :].astype(jnp.float32) + chip_ref[here, :].astype(jnp.float32)
        updated, first_new[here, :], second_new[here, :] = adam_step(
            gradient, weight_ref[there, :], first_ref[there, :], second_ref[there, :]
        )
        weight_new[here, width:] = updated[:, width:]
        weight_new[here, :width] = MIX_SHARE * updated[:, :width] + (1.0 - MIX_SHARE) * outer_ref[here, :]
        for new, out in ((weight_new, weight_out), (first_new, first_out), (second_new, second_out)):
            stores.append(
                pltpu.make_async_copy(
                    new.at[pl.ds(i * BLOCK, BLOCK)], out.at[pl.ds(last + i * BLOCK, BLOCK)], sems.at[len(stores)]
                )
            )
            stores[-1].start()
    for copy in stores:
        copy.wait()


def last_step(weight, first, second, own, core, chip, outer, outs):
    count, width = chip.shape
    operands = [weight, first, second, own, core, chip, outer]
    return pl.pallas_call(
        last_kernel,
        out_shape=[jax.ShapeDtypeStruct(a.shape, a.dtype) for a in (weight, first, second)],
        in_specs=[VMEM] * len(operands) + [ANY] * 3,
        out_specs=[ANY] * 3,
        input_output_aliases={len(operands) + i: i for i in range(3)},
        scratch_shapes=[
            pltpu.VMEM((count, width), weight.dtype),
            pltpu.VMEM((count, width), first.dtype),
            pltpu.VMEM((count, width), second.dtype),
            pltpu.SemaphoreType.DMA((3 * (count // BLOCK),)),
        ],
        compiler_params=params(),
        cost_estimate=cost(0),
    )(*operands, *outs)


def swap(x, axis, flip):
    size = lax.axis_size(axis)
    return lax.ppermute(x, axis, [(i, i ^ flip) for i in range(size)])


def island_groups(islands):
    inner = 2
    while inner * inner * 4 <= islands:
        inner *= 2
    return islands // inner, inner


def add_kernel(mine_ref, other_ref, out_ref):
    out_ref[...] = (mine_ref[...] + other_ref[...].astype(jnp.float32)).astype(out_ref.dtype)


def start_kernel(out_ref):
    out_ref[...] = jnp.zeros_like(out_ref)


def join_kernel(others, code_ref, *refs):
    total = code_ref[...]
    for other in refs[:others]:
        total += other[...] & -8
    refs[-1][...] = total


def local(acts, cotangent, weight, first, second, outer_weight, outer_momentum, mantissas, exponents):
    acts, cot, weight, first, second = acts[0], cotangent[0], weight[0], first[0], second[0]
    mant, lines = mantissas[0], exponents[0].reshape(-1, 128)
    rows, width = weight.shape
    bf16 = jnp.bfloat16
    islands = lax.axis_size("replica")
    parts, group = island_groups(islands)
    length, head = rows // parts, mant.shape[1]
    unit = rows // 8
    chunks = ((0, 2 * unit), (2 * unit, 4 * unit), (6 * unit, 2 * unit))
    late = rows - chunks[0][1]

    ready = pl.pallas_call(
        start_kernel,
        out_shape=jax.ShapeDtypeStruct((8, 128), jnp.int32),
        out_specs=VMEM,
        compiler_params=params(),
        cost_estimate=cost(1),
    )()
    all_lines = [lines] + [swap(lines, "replica", k) for k in range(1, group)]

    theirs = [product(acts, cot, 3, *chunks[0], rows, bf16, after=(ready,))]
    theirs.append(product(acts, cot, 3, chunks[1][0], late, rows, bf16, after=theirs, us=FILL))
    shares = [swap(part, "fsdp", 1) for part in theirs]
    mine = product(acts, cot, 2, *chunks[0], rows, jnp.float32, after=theirs[1:], us=FILL)
    sends = [
        pl.pallas_call(
            add_kernel,
            out_shape=jax.ShapeDtypeStruct(mine.shape, bf16),
            in_specs=[VMEM, VMEM],
            out_specs=VMEM,
            compiler_params=params(),
            cost_estimate=cost(0),
        )(mine, shares[0])
    ]
    codes = pl.pallas_call(
        functools.partial(code_kernel, parts, group),
        out_shape=[jax.ShapeDtypeStruct((length, head), jnp.int16)] * parts,
        in_specs=[VMEM] * (1 + group) + [ANY],
        out_specs=[VMEM] * parts,
        compiler_params=params(),
        cost_estimate=cost(0),
    )(mant, *all_lines, sends[0])
    sends.append(product(acts, cot, 2, *chunks[1], rows, bf16, shares[1], after=sends[:1], us=FILL))

    core = product(acts, cot, 1, 0, rows, rows, bf16, after=sends[1:], us=FILL)
    codes = list(codes)
    codes[1], _ = lax.optimization_barrier((codes[1], sends[1]))
    codes = codes[:1] + [swap(codes[k], "replica", k * group) for k in range(parts - 1, 0, -1)]
    wide = jnp.int16 if islands * 128 * 8 <= 2 ** 15 else jnp.int32
    code = pl.pallas_call(
        functools.partial(align_kernel, parts),
        out_shape=jax.ShapeDtypeStruct((length, head), wide),
        in_specs=[VMEM] * parts + [ANY],
        out_specs=VMEM,
        compiler_params=params(),
        cost_estimate=cost(0),
    )(*codes, core)
    core = swap(core, "fsdp", 1)
    others = [swap(code, "replica", k) for k in range(1, group)]
    skip = chunks[2][0] - chunks[1][0]
    sends.append(product(acts, cot, 2, *chunks[2], rows, bf16, shares[1], skip, after=(code,)))
    arrived = [swap(part, "fsdp", 2) for part in sends]
    own = product(acts, cot, 0, 0, rows, rows, jnp.float32, after=(code,), us=FILL)
    total = pl.pallas_call(
        functools.partial(join_kernel, group - 1),
        out_shape=jax.ShapeDtypeStruct((length, head), wide),
        in_specs=[VMEM] * group + [ANY],
        out_specs=VMEM,
        compiler_params=params(),
        cost_estimate=cost(0),
    )(code, *others, own)
    received = {k: swap(total, "replica", k * group) for k in range(parts - 1, 0, -1)}
    codes = [total] + [received[k] for k in range(1, parts)]

    outs, heads = (), []
    for (row, _), part in zip(chunks[:-1], arrived):
        *outs, part_head = adam(
            own, core, part, weight, first, second, row, head, outs, us=FILL, after=() if outs else (total,)
        )
        heads.append(part_head)
    weight_new, outer_new, momentum_new, tail = outer_step(
        outs[0], outer_weight, outer_momentum, codes, heads, group, islands
    )
    weight_new, first_new, second_new = last_step(
        weight, first, second, own, core, arrived[-1], tail, (weight_new, *outs[1:])
    )
    return (weight_new[None], first_new[None], second_new[None], outer_new, momentum_new)


def solution(mesh):
    tall = P("replica", "fsdp", None)
    fragment = P("fsdp", None)
    in_specs = (tall, tall, tall, tall, tall, fragment, fragment, tall, P("replica", "fsdp"))
    out_specs = (tall, tall, tall, fragment, fragment)
    return jax.shard_map(local, mesh=mesh, in_specs=in_specs, out_specs=out_specs, check_vma=False)
```

```python
import functools

import jax
import jax.numpy as jnp
from jax import lax
from jax.experimental import pallas as pl
from jax.experimental.pallas import tpu as pltpu
from jax.sharding import PartitionSpec as P

BETA_ONE = 0.9
BETA_TWO = 0.95
LEARN_RATE = 0.001
DECAY_RATE = 0.1
ADAM_EPSILON = 1e-08
OUTER_RATE = 0.7
OUTER_MOMENTUM = 0.9
MIX_SHARE = 0.5
LEAST_EXPONENT = -10

ANY = pl.BlockSpec(memory_space=pl.ANY)
VMEM = pl.BlockSpec(memory_space=pltpu.VMEM)
BLOCK = 128
FILL = 20
LIMIT = 32 * 1024 * 1024


def params():
    return pltpu.CompilerParams(vmem_limit_bytes=LIMIT)


def cost(us):
    return pl.CostEstimate(flops=int(us * 1.15e9), bytes_accessed=0, transcendentals=0)


def token_product(tokens, cot):
    return lax.dot_general(tokens, cot, (((0,), (0,)), ((), ())), preferred_element_type=jnp.float32)


def product_kernel(flip, row, rows, summed, skip, acts_ref, cot_ref, *refs):
    out_ref = refs[-1]
    owner = lax.axis_index("fsdp") ^ flip
    for at in range(0, out_ref.shape[0], 128):
        size = min(128, out_ref.shape[0] - at)
        cols = pl.ds(pl.multiple_of(owner * rows + row + at, 128), size)
        total = token_product(acts_ref[:, cols], cot_ref[...])
        if summed:
            total = total + refs[0][skip + at:skip + at + size, :].astype(jnp.float32)
        out_ref[at:at + size, :] = total.astype(out_ref.dtype)


def product(acts, cot, flip, row, count, rows, dtype, other=None, skip=0, after=(), us=0):
    width = cot.shape[1]
    shares = () if other is None else (other,)
    return pl.pallas_call(
        functools.partial(product_kernel, flip, row, rows, len(shares), skip),
        out_shape=jax.ShapeDtypeStruct((count, width), dtype),
        in_specs=[VMEM] * (2 + len(shares)) + [ANY] * len(after),
        out_specs=VMEM,
        compiler_params=params(),
        cost_estimate=cost(us),
    )(acts, cot, *shares, *after)


def adam_step(gradient, weight, first, second):
    moment_one = BETA_ONE * first.astype(jnp.float32) + (1.0 - BETA_ONE) * gradient
    moment_two = BETA_TWO * second.astype(jnp.float32) + (1.0 - BETA_TWO) * gradient * gradient
    root = moment_two * lax.rsqrt(moment_two)
    step = moment_one / (root + ADAM_EPSILON)
    updated = weight - LEARN_RATE * (step + DECAY_RATE * weight)
    return updated, moment_one.astype(first.dtype), moment_two.astype(second.dtype)


def adam_kernel(row, ahead, own_ref, core_ref, chip_ref, weight_ref, first_ref, second_ref, *refs):
    weight_out, first_out, second_out, head_out, *base, weight_new, first_new, second_new, sems = refs[-8 - (ahead > 0):]
    count = chip_ref.shape[0]
    stores = []
    for i in range(count // BLOCK):
        here, there = slice(i * BLOCK, (i + 1) * BLOCK), slice(row + i * BLOCK, row + (i + 1) * BLOCK)
        gradient = own_ref[there, :] + core_ref[there, :].astype(jnp.float32) + chip_ref[here, :].astype(jnp.float32)
        updated, first_new[here, :], second_new[here, :] = adam_step(
            gradient, weight_ref[there, :], first_ref[there, :], second_ref[there, :]
        )
        weight_new[here, :] = updated
        head_out[here, :] = updated[:, : head_out.shape[1]]
        for new, out in ((weight_new, weight_out), (first_new, first_out), (second_new, second_out)):
            stores.append(
                pltpu.make_async_copy(
                    new.at[pl.ds(i * BLOCK, BLOCK)], out.at[pl.ds(row + i * BLOCK, BLOCK)], sems.at[len(stores)]
                )
            )
            stores[-1].start()
    if ahead:
        base[0][...] = own_ref[-ahead:, :] + core_ref[-ahead:, :].astype(jnp.float32)
    for copy in stores:
        copy.wait()


def adam(own, core, chip, weight, first, second, row, head, outs=(), us=0, after=(), ahead=0):
    count, width = chip.shape
    operands = [own, core, chip, weight, first, second]
    return pl.pallas_call(
        functools.partial(adam_kernel, row, ahead),
        out_shape=[jax.ShapeDtypeStruct(a.shape, a.dtype) for a in (weight, first, second)]
        + [jax.ShapeDtypeStruct((count, head), weight.dtype)]
        + [jax.ShapeDtypeStruct((ahead, width), jnp.float32)] * (ahead > 0),
        in_specs=[VMEM] * len(operands) + [ANY] * (len(outs) + len(after)),
        out_specs=[ANY] * 3 + [VMEM] * (1 + (ahead > 0)),
        input_output_aliases={len(operands) + i: i for i in range(len(outs))},
        scratch_shapes=[
            pltpu.VMEM((count, width), weight.dtype),
            pltpu.VMEM((count, width), first.dtype),
            pltpu.VMEM((count, width), second.dtype),
            pltpu.SemaphoreType.DMA((3 * (count // BLOCK),)),
        ],
        compiler_params=params(),
        cost_estimate=cost(us),
    )(*operands, *outs, *after)


def by_row(exps_ref, at):
    line = exps_ref[pl.ds(at, 1), :]
    return jnp.broadcast_to(line, (128, 128)).T


def code_kernel(parts, group, mant_ref, *refs):
    exps, outs = refs[:group], refs[len(refs) - parts:]
    where = lax.axis_index("replica") // group
    length = outs[0].shape[0]
    for k in range(parts):
        row = (where ^ k) * length
        for i in range(length // 128):
            line = row // 128 + i
            own = by_row(exps[0], line)
            top = own
            for other in exps[1:]:
                top = jnp.maximum(top, by_row(other, line))
            mant = mant_ref[pl.ds(pl.multiple_of(row + i * 128, 128), 128), :]
            code = mant * 64 + (own - LEAST_EXPONENT) * 8 + (top - LEAST_EXPONENT)
            outs[k][i * 128:(i + 1) * 128, :] = code.astype(outs[k].dtype)


def align_kernel(parts, *refs):
    codes = [r[...].astype(jnp.int32) for r in refs[:parts]]
    top = functools.reduce(jnp.maximum, [c & 7 for c in codes])
    total = sum(jnp.right_shift(c >> 6, top - ((c >> 3) & 7)) for c in codes)
    refs[-1][...] = (total * 8 + top).astype(refs[-1].dtype)


def outer_kernel(group, islands, parts, early, ow_ref, om_ref, *refs):
    codes, heads = refs[:parts], refs[parts:parts + early]
    weight_out, outer_out, momentum_out, tail_out, outer, momentum, mixed, sems = refs[parts + early + 1:]
    where = lax.axis_index("replica") // group
    length = codes[0].shape[0]
    last, width = mixed.shape
    stores = []

    def store(source, target):
        stores.append(pltpu.make_async_copy(source, target, sems.at[len(stores)]))
        stores[-1].start()

    for k in range(parts):
        at = pl.ds(pl.multiple_of((where ^ k) * length, length), length)
        code = codes[k][...].astype(jnp.int32)
        scale = jnp.left_shift(1, code & 7).astype(jnp.float32) * (2.0 ** LEAST_EXPONENT / islands)
        pseudo = (code >> 3).astype(jnp.float32) * scale
        moved = OUTER_MOMENTUM * om_ref[at, :] + pseudo
        momentum[at, :] = moved
        outer[at, :] = ow_ref[at, :] - OUTER_RATE * (pseudo + OUTER_MOMENTUM * moved)
        store(momentum.at[at], momentum_out.at[at])
        store(outer.at[at], outer_out.at[at])
    row = 0
    for head in heads:
        at = slice(row, row + head.shape[0])
        mixed[at, :] = MIX_SHARE * head[...] + (1.0 - MIX_SHARE) * outer[at, :]
        row += head.shape[0]
    store(mixed, weight_out.at[pl.ds(0, last), pl.ds(0, width)])
    tail_out[...] = outer[last:, :]
    for copy in stores:
        copy.wait()


def outer_step(weight, outer_weight, outer_momentum, codes, heads, group, islands):
    parts, early = len(codes), len(heads)
    rows, width = outer_weight.shape
    last = sum(h.shape[0] for h in heads)
    operands = [outer_weight, outer_momentum, *codes, *heads]
    return pl.pallas_call(
        functools.partial(outer_kernel, group, islands, parts, early),
        out_shape=[jax.ShapeDtypeStruct(a.shape, a.dtype) for a in (weight, outer_weight, outer_momentum)]
        + [jax.ShapeDtypeStruct((rows - last, width), jnp.float32)],
        in_specs=[VMEM] * len(operands) + [ANY],
        out_specs=[ANY] * 3 + [VMEM],
        input_output_aliases={len(operands): 0},
        scratch_shapes=[
            pltpu.VMEM((rows, width), jnp.float32),
            pltpu.VMEM((rows, width), jnp.float32),
            pltpu.VMEM((last, width), jnp.float32),
            pltpu.SemaphoreType.DMA((2 * parts + 1,)),
        ],
        compiler_params=params(),
        cost_estimate=cost(0),
    )(*operands, weight)


def last_kernel(weight_ref, first_ref, second_ref, base_ref, chip_ref, outer_ref, *refs):
    weight_out, first_out, second_out, weight_new, first_new, second_new, sems = refs[3:]
    count = chip_ref.shape[0]
    last = weight_ref.shape[0] - count
    width = outer_ref.shape[1]
    stores = []
    for i in range(count // BLOCK):
        here, there = slice(i * BLOCK, (i + 1) * BLOCK), slice(last + i * BLOCK, last + (i + 1) * BLOCK)
        gradient = base_ref[here, :] + chip_ref[here, :].astype(jnp.float32)
        updated, first_new[here, :], second_new[here, :] = adam_step(
            gradient, weight_ref[there, :], first_ref[there, :], second_ref[there, :]
        )
        weight_new[here, width:] = updated[:, width:]
        weight_new[here, :width] = MIX_SHARE * updated[:, :width] + (1.0 - MIX_SHARE) * outer_ref[here, :]
        for new, out in ((weight_new, weight_out), (first_new, first_out), (second_new, second_out)):
            stores.append(
                pltpu.make_async_copy(
                    new.at[pl.ds(i * BLOCK, BLOCK)], out.at[pl.ds(last + i * BLOCK, BLOCK)], sems.at[len(stores)]
                )
            )
            stores[-1].start()
    for copy in stores:
        copy.wait()


def last_step(weight, first, second, base, chip, outer, outs):
    count, width = chip.shape
    operands = [weight, first, second, base, chip, outer]
    return pl.pallas_call(
        last_kernel,
        out_shape=[jax.ShapeDtypeStruct(a.shape, a.dtype) for a in (weight, first, second)],
        in_specs=[VMEM] * len(operands) + [ANY] * 3,
        out_specs=[ANY] * 3,
        input_output_aliases={len(operands) + i: i for i in range(3)},
        scratch_shapes=[
            pltpu.VMEM((count, width), weight.dtype),
            pltpu.VMEM((count, width), first.dtype),
            pltpu.VMEM((count, width), second.dtype),
            pltpu.SemaphoreType.DMA((3 * (count // BLOCK),)),
        ],
        compiler_params=params(),
        cost_estimate=cost(0),
    )(*operands, *outs)


def swap(x, axis, flip):
    size = lax.axis_size(axis)
    return lax.ppermute(x, axis, [(i, i ^ flip) for i in range(size)])


def island_groups(islands):
    inner = 2
    while inner * inner * 4 <= islands:
        inner *= 2
    return islands // inner, inner


def add_kernel(mine_ref, other_ref, out_ref):
    out_ref[...] = (mine_ref[...] + other_ref[...].astype(jnp.float32)).astype(out_ref.dtype)


def start_kernel(out_ref):
    out_ref[...] = jnp.zeros_like(out_ref)


def join_kernel(others, code_ref, *refs):
    total = code_ref[...]
    for other in refs[:others]:
        total += other[...] & -8
    refs[-1][...] = total


def local(acts, cotangent, weight, first, second, outer_weight, outer_momentum, mantissas, exponents):
    acts, cot, weight, first, second = acts[0], cotangent[0], weight[0], first[0], second[0]
    mant, lines = mantissas[0], exponents[0].reshape(-1, 128)
    rows, width = weight.shape
    bf16 = jnp.bfloat16
    islands = lax.axis_size("replica")
    parts, group = island_groups(islands)
    length, head = rows // parts, mant.shape[1]
    unit = rows // 8
    chunks = ((0, 2 * unit), (2 * unit, 4 * unit), (6 * unit, 2 * unit))
    late = rows - chunks[0][1]

    ready = pl.pallas_call(
        start_kernel,
        out_shape=jax.ShapeDtypeStruct((8, 128), jnp.int32),
        out_specs=VMEM,
        compiler_params=params(),
        cost_estimate=cost(1),
    )()
    all_lines = [lines] + [swap(lines, "replica", k) for k in range(1, group)]

    theirs = [product(acts, cot, 3, *chunks[0], rows, bf16, after=(ready,))]
    theirs.append(product(acts, cot, 3, chunks[1][0], late, rows, bf16, after=theirs, us=FILL))
    shares = [swap(part, "fsdp", 1) for part in theirs]
    mine = product(acts, cot, 2, *chunks[0], rows, jnp.float32, after=theirs[1:], us=FILL)
    sends = [
        pl.pallas_call(
            add_kernel,
            out_shape=jax.ShapeDtypeStruct(mine.shape, bf16),
            in_specs=[VMEM, VMEM],
            out_specs=VMEM,
            compiler_params=params(),
            cost_estimate=cost(0),
        )(mine, shares[0])
    ]
    codes = pl.pallas_call(
        functools.partial(code_kernel, parts, group),
        out_shape=[jax.ShapeDtypeStruct((length, head), jnp.int16)] * parts,
        in_specs=[VMEM] * (1 + group) + [ANY],
        out_specs=[VMEM] * parts,
        compiler_params=params(),
        cost_estimate=cost(0),
    )(mant, *all_lines, sends[0])
    sends.append(product(acts, cot, 2, *chunks[1], rows, bf16, shares[1], after=sends[:1], us=FILL))

    core = product(acts, cot, 1, 0, rows, rows, bf16, after=sends[1:], us=FILL)
    codes = list(codes)
    codes[1], _ = lax.optimization_barrier((codes[1], sends[1]))
    codes = codes[:1] + [swap(codes[k], "replica", k * group) for k in range(parts - 1, 0, -1)]
    wide = jnp.int16 if islands * 128 * 8 <= 2 ** 15 else jnp.int32
    code = pl.pallas_call(
        functools.partial(align_kernel, parts),
        out_shape=jax.ShapeDtypeStruct((length, head), wide),
        in_specs=[VMEM] * parts + [ANY],
        out_specs=VMEM,
        compiler_params=params(),
        cost_estimate=cost(0),
    )(*codes, core)
    core = swap(core, "fsdp", 1)
    others = [swap(code, "replica", k) for k in range(1, group)]
    skip = chunks[2][0] - chunks[1][0]
    sends.append(product(acts, cot, 2, *chunks[2], rows, bf16, shares[1], skip, after=(code,)))
    arrived = [swap(part, "fsdp", 2) for part in sends]
    own = product(acts, cot, 0, 0, rows, rows, jnp.float32, after=(code,), us=FILL)
    total = pl.pallas_call(
        functools.partial(join_kernel, group - 1),
        out_shape=jax.ShapeDtypeStruct((length, head), wide),
        in_specs=[VMEM] * group + [ANY],
        out_specs=VMEM,
        compiler_params=params(),
        cost_estimate=cost(0),
    )(code, *others, own)
    received = {k: swap(total, "replica", k * group) for k in range(parts - 1, 0, -1)}
    codes = [total] + [received[k] for k in range(1, parts)]

    *outs, first_head, base = adam(
        own, core, arrived[0], weight, first, second, 0, head, us=FILL, after=(total,), ahead=chunks[2][1]
    )
    *outs, second_head = adam(own, core, arrived[1], weight, first, second, chunks[1][0], head, outs, us=FILL)
    heads = [first_head, second_head]
    weight_new, outer_new, momentum_new, tail = outer_step(
        outs[0], outer_weight, outer_momentum, codes, heads, group, islands
    )
    weight_new, first_new, second_new = last_step(
        weight, first, second, base, arrived[-1], tail, (weight_new, *outs[1:])
    )
    return (weight_new[None], first_new[None], second_new[None], outer_new, momentum_new)


def solution(mesh):
    tall = P("replica", "fsdp", None)
    fragment = P("fsdp", None)
    in_specs = (tall, tall, tall, tall, tall, fragment, fragment, tall, P("replica", "fsdp"))
    out_specs = (tall, tall, tall, fragment, fragment)
    return jax.shard_map(local, mesh=mesh, in_specs=in_specs, out_specs=out_specs, check_vma=False)
```
